256 devices in a mesh: prompt: 16 (over y, x_hi, core), seq: 16 (over z, x_lo).
Axes of the slice: x: 4 (x_hi: 2, x_lo: 2; x = x_hi * 2 + x_lo), y: 4, z: 8, core: 2. Of those that a mesh axis runs over, the one named last changes fastest.
Arguments:
- queries: bfloat16 [16, 2048, 4096], P('prompt', 'seq'), may hold values from -8 to 8
- self_keys: bfloat16 [16, 2048, 4096], P('prompt', 'seq'), may hold values from -8 to 8
- self_values: bfloat16 [16, 2048, 4096], P('prompt', 'seq'), may hold values from -6 to 6
- cross_queries: bfloat16 [16, 2048, 4096], P('prompt', 'seq')
- context: bfloat16 [16, 512, 5120], P('prompt', 'seq')
- key_weight: bfloat16 [5120, 4096], P('prompt', 'seq')
- value_weight: bfloat16 [5120, 4096], P('prompt', 'seq'), may hold values from -0.078125 to 0.078125
- lengths: int32 [16], P('prompt'), may hold values from 64 to 512, as said below
Outputs:
- attended: bfloat16 [16, 2048, 4096], P('prompt', 'seq')
The draws below stay inside these ranges and needn't reach their ends.
Inputs may be any that keep to these rules, and one draw needn't show every extreme that they name: `lengths`: each prompt's number of text tokens; some prompt has all 512.
All inputs are finite; a program needn't handle non-finite values.
Results may differ from the reference program's by a relative error of at most 0.007.
Values may be sent and summed in bfloat16 or wider, within the bound.
No kernel may reach another device: no remote copies, remote signals or barrier semaphores. Data moves between devices by JAX's collectives and lax.ppermute only.
A program may use at most 64 MiB of HBM per device.

```python
import math
import jax
import jax.numpy as jnp
from jax import lax

D = 5120
HD = 128
HEADS = 32
TXT = 512
PROMPTS = 16
SEQ_LEN = 2048
HW = 4096


def self_pair(key):
    query_seed, key_seed = jax.random.split(jax.random.fold_in(key, 7), 2)
    full_shape = (PROMPTS, SEQ_LEN, HEADS * HD)
    query_draw = jnp.clip(jax.random.normal(query_seed, full_shape, jnp.float32), -6.0, 6.0)
    key_draw = jnp.clip(jax.random.normal(key_seed, full_shape, jnp.float32), -6.0, 6.0)
    return (query_draw, key_draw)


def cross_parts(key):
    weight_seed, context_seed, query_seed = jax.random.split(jax.random.fold_in(key, 13), 3)
    weight_draw = jax.random.normal(weight_seed, (D, HEADS * HD), jnp.float32) / math.sqrt(D)
    context_draw = jnp.clip(jax.random.normal(context_seed, (PROMPTS, TXT, D), jnp.float32), -6.0, 6.0)
    query_draw = jnp.clip(jax.random.normal(query_seed, (PROMPTS, SEQ_LEN, HEADS * HD), jnp.float32), -6.0, 6.0)
    return (weight_draw, context_draw, query_draw)


def draw_queries(key, part):
    return self_pair(key)[0].astype(jnp.bfloat16)


def draw_self_keys(key, part):
    return self_pair(key)[1].astype(jnp.bfloat16)


def draw_key_weight(key, part):
    return cross_parts(key)[0].astype(jnp.bfloat16)


def draw_context(key, part):
    return cross_parts(key)[1].astype(jnp.bfloat16)


def draw_cross_queries(key, part):
    return cross_parts(key)[2].astype(jnp.bfloat16)


def draw_lengths(key, part):
    first_seed, second_seed, longest_seed = jax.random.split(jax.random.fold_in(key, 29), 3)
    first_draw = jax.random.randint(first_seed, (PROMPTS,), TXT // 8, TXT + 1)
    second_draw = jax.random.randint(second_seed, (PROMPTS,), TXT // 8, TXT + 1)
    shorter = jnp.minimum(first_draw, second_draw)
    longest = jax.random.randint(longest_seed, (), 0, PROMPTS)
    return jnp.where(jnp.arange(PROMPTS) == longest, TXT, shorter).astype(jnp.int32)


def steps_of(rng, dims, cuts, smallest, high):
    gain, own = 1.0, jax.random.fold_in(rng, 6)
    for axis_at, blocks in cuts:
        draws = jnp.exp(jax.random.uniform(jax.random.fold_in(own, axis_at), (blocks,), jnp.float32, smallest / len(cuts), high / len(cuts)))
        gain = gain * jnp.repeat(draws, dims[axis_at] // blocks).reshape([-1 if axis == axis_at else 1 for axis in range(len(dims))])
    return gain


def gaussian(stream_key, dims, scale, bound, shards=(), kind=jnp.bfloat16):
    values = scale * jax.random.normal(stream_key, dims, jnp.float32)
    if shards:
        values = values * steps_of(stream_key, dims, shards, -0.22, 0.18)
    return jnp.clip(values, -bound, bound).astype(kind)


def setup_inputs(seed: int = 0) -> dict:
    splits = jax.random.split(jax.random.key(seed), 9)
    return {
        "queries": draw_queries(jax.random.fold_in(splits[8], 71), 0),
        "self_keys": draw_self_keys(jax.random.fold_in(splits[8], 71), 0),
        "self_values": gaussian(splits[2], (PROMPTS, SEQ_LEN, HW), 1.0, 6.0, ((0, 16), (1, 16))),
        "cross_queries": draw_cross_queries(jax.random.fold_in(splits[8], 71), 0),
        "context": draw_context(jax.random.fold_in(splits[8], 71), 0),
        "key_weight": draw_key_weight(jax.random.fold_in(splits[8], 71), 0),
        "value_weight": gaussian(splits[6], (D, HW), D ** -0.5, 0.078125, ((0, 16), (1, 16))),
        "lengths": draw_lengths(jax.random.fold_in(splits[8], 71), 0),
    }


def attend_head(query_rows, key_rows, value_rows, usable):
    scaling = 1.0 / math.sqrt(HD)
    scores = jnp.dot(query_rows, key_rows.T, preferred_element_type=jnp.float32) * scaling
    row_max = lax.optimization_barrier(jnp.max(jnp.where(usable[None, :], scores, -jnp.inf), axis=1))
    shifted = jnp.where(usable[None, :], scores, row_max[:, None]) - row_max[:, None]
    weights = jnp.where(usable[None, :], jnp.exp(shifted), jnp.zeros_like(shifted))
    totals = lax.optimization_barrier(jnp.sum(weights, axis=1))
    mixed = jnp.dot(weights.astype(jnp.bfloat16), value_rows, preferred_element_type=jnp.float32)
    return (mixed / totals[:, None]).astype(jnp.bfloat16)

def by_head(matrix):
    return matrix.reshape(matrix.shape[0], HEADS, HD).transpose(1, 0, 2)

def reference(queries, self_keys, self_values, cross_queries, context, key_weight, value_weight, lengths):

    def one_prompt(inputs):
        query_all, key_all, value_all, cross_all, context_rows, length = inputs
        text_keys = jnp.dot(context_rows, key_weight, preferred_element_type=jnp.float32).astype(jnp.bfloat16)
        text_values = jnp.dot(context_rows, value_weight, preferred_element_type=jnp.float32).astype(jnp.bfloat16)
        every_token = jnp.ones((SEQ_LEN,), dtype=bool)
        text_usable = jnp.arange(TXT, dtype=jnp.int32) < length

        def one_head(parts):
            query_head, key_head, value_head, cross_head, text_key_head, text_value_head = parts
            self_part = attend_head(query_head, key_head, value_head, every_token)
            cross_part = attend_head(cross_head, text_key_head, text_value_head, text_usable)
            return (self_part.astype(jnp.float32) + cross_part.astype(jnp.float32)).astype(jnp.bfloat16)
        mixed = lax.map(one_head, (by_head(query_all), by_head(key_all), by_head(value_all), by_head(cross_all), by_head(text_keys), by_head(text_values)))
        return mixed.transpose(1, 0, 2).reshape(SEQ_LEN, HEADS * HD)
    return lax.map(one_prompt, (queries, self_keys, self_values, cross_queries, context, lengths))
```

```python
import math

import jax
import jax.numpy as jnp
from jax import lax
from jax.experimental import pallas as pl
from jax.experimental.pallas import tpu as pltpu
from jax.sharding import PartitionSpec as P

HD = 128
EXP2_SCALE = math.log2(math.e) / math.sqrt(HD)


def softmax_mix(query, keys, values, usable):
    scores = lax.dot_general(
        query, keys, (((1,), (1,)), ((), ())), preferred_element_type=jnp.float32
    )
    if usable is not None:
        scores = jnp.where(usable, scores, -jnp.inf)
    row_max = jnp.max(scores, axis=1, keepdims=True)
    weights = jnp.exp2((scores - row_max) * EXP2_SCALE)
    totals = jnp.sum(weights, axis=1, keepdims=True)
    mixed = jnp.dot(weights.astype(jnp.bfloat16), values, preferred_element_type=jnp.float32)
    return mixed / totals


def attend_kernel(length_ref, q_ref, k_ref, v_ref, cq_ref, tk_ref, tv_ref, out_ref):
    text_slots = tk_ref.shape[0]
    usable = lax.broadcasted_iota(jnp.int32, (1, text_slots), 1) < length_ref[0]
    for head in range(q_ref.shape[1] // HD):
        cols = slice(head * HD, (head + 1) * HD)
        self_out = softmax_mix(q_ref[:, cols], k_ref[:, cols], v_ref[:, cols], None)
        cross_out = softmax_mix(cq_ref[:, cols], tk_ref[:, cols], tv_ref[:, cols], usable)
        out_ref[:, cols] = (
            self_out.astype(jnp.bfloat16).astype(jnp.float32)
            + cross_out.astype(jnp.bfloat16).astype(jnp.float32)
        ).astype(jnp.bfloat16)


def attend(length, q, k, v, cq, tk, tv):
    rows, width = q.shape
    block = math.gcd(rows, 256)
    row_spec = pl.BlockSpec((block, width), lambda i: (i, 0))

    def whole(array):
        return pl.BlockSpec(array.shape, lambda i: (0, 0))

    pairs = rows * width * (k.shape[0] + tk.shape[0])
    return pl.pallas_call(
        attend_kernel,
        grid=(rows // block,),
        in_specs=[
            pl.BlockSpec(memory_space=pltpu.SMEM),
            row_spec,
            whole(k),
            whole(v),
            row_spec,
            whole(tk),
            whole(tv),
        ],
        out_specs=row_spec,
        out_shape=jax.ShapeDtypeStruct((rows, width), jnp.bfloat16),
        compiler_params=pltpu.CompilerParams(vmem_limit_bytes=40 << 20),
        cost_estimate=pl.CostEstimate(
            flops=4 * pairs,
            bytes_accessed=10 * rows * width,
            transcendentals=pairs // HD,
        ),
        name="attend",
    )(length, q, k, v, cq, tk, tv)


def body(
    queries, self_keys, self_values, cross_queries, context, key_weight, value_weight, lengths
):
    def to_heads(rows):
        return lax.all_to_all(rows, "seq", split_axis=1, concat_axis=0, tiled=True)

    text_full = lax.all_gather(context[0], "seq", axis=0, tiled=True)
    key_full = lax.all_gather(key_weight, "prompt", axis=0, tiled=True)
    value_full = lax.all_gather(value_weight, "prompt", axis=0, tiled=True)
    q = to_heads(queries[0])
    k = to_heads(self_keys[0])
    v = to_heads(self_values[0])
    cq = to_heads(cross_queries[0])
    tk = jnp.dot(text_full, key_full, preferred_element_type=jnp.float32).astype(jnp.bfloat16)
    tv = jnp.dot(text_full, value_full, preferred_element_type=jnp.float32).astype(jnp.bfloat16)
    attended = attend(lengths, q, k, v, cq, tk, tv)
    return lax.all_to_all(attended, "seq", split_axis=0, concat_axis=1, tiled=True)[None]


def solution(mesh):
    in_specs = (
        P("prompt", "seq", None),
        P("prompt", "seq", None),
        P("prompt", "seq", None),
        P("prompt", "seq", None),
        P("prompt", "seq", None),
        P("prompt", "seq"),
        P("prompt", "seq"),
        P("prompt"),
    )
    out_specs = P("prompt", "seq", None)
    return jax.shard_map(body, mesh=mesh, in_specs=in_specs, out_specs=out_specs, check_vma=False)
```

```python
import math

import jax
import jax.numpy as jnp
from jax import lax
from jax.experimental import pallas as pl
from jax.experimental.pallas import tpu as pltpu
from jax.sharding import PartitionSpec as P

HD = 128
EXP2_SCALE = math.log2(math.e) / math.sqrt(HD)
Y, XH, CORE = 4, 2, 2
Z, XL = 8, 2


def y_shift(step):
    block = XH * CORE
    return [(p, (p + step * block) % (Y * block)) for p in range(Y * block)]


def z_shift(step):
    return [(s, (s + step * XL) % (Z * XL)) for s in range(Z * XL)]


CORE_SWAP = [(p, p ^ 1) for p in range(Y * XH * CORE)]
XL_SWAP = [(s, s ^ 1) for s in range(Z * XL)]
REGROUP_A = [(4 * y + a, 4 * y + b) for y in range(Y) for a, b in ((0, 2), (2, 3), (3, 1), (1, 0))]
REGROUP_B = [(4 * y + a, 4 * y + b) for y in range(Y) for a, b in ((1, 2), (2, 1))]


def pack_kernel(*refs):
    out_ref = refs[-1]
    width = refs[0].shape[1]
    for place, ref in enumerate(refs[:-1]):
        out_ref[0, :, place * width : (place + 1) * width] = ref[...]


def pack(arrays, parts):
    rows, columns = arrays[0].shape
    width = columns // parts
    return pl.pallas_call(
        pack_kernel,
        grid=(parts,),
        in_specs=[pl.BlockSpec((rows, width), lambda i: (0, i)) for _ in arrays],
        out_specs=pl.BlockSpec((1, rows, width * len(arrays)), lambda i: (i, 0, 0)),
        out_shape=jax.ShapeDtypeStruct((parts, rows, width * len(arrays)), jnp.bfloat16),
        cost_estimate=pl.CostEstimate(
            flops=0, bytes_accessed=4 * rows * columns * len(arrays), transcendentals=0
        ),
        name="pack",
    )(*arrays)


def unpack_kernel(in_ref, out_ref):
    out_ref[...] = in_ref[0]


def unpack(blocks):
    parts, rows, width = blocks.shape
    return pl.pallas_call(
        unpack_kernel,
        grid=(parts,),
        in_specs=[pl.BlockSpec((1, rows, width), lambda i: (i, 0, 0))],
        out_specs=pl.BlockSpec((rows, width), lambda i: (0, i)),
        out_shape=jax.ShapeDtypeStruct((rows, parts * width), jnp.bfloat16),
        name="unpack",
    )(blocks)


def softmax_mix(query, keys, values, bias):
    scores = lax.dot_general(
        query, keys, (((1,), (1,)), ((), ())), preferred_element_type=jnp.float32
    )
    if bias is not None:
        scores = scores + bias
    row_max = jnp.max(scores, axis=1, keepdims=True)
    weights = jnp.exp2((scores - row_max) * EXP2_SCALE)
    totals = jnp.sum(weights, axis=1, keepdims=True)
    mixed = jnp.dot(weights.astype(jnp.bfloat16), values, preferred_element_type=jnp.float32)
    return mixed / totals


def self_kernel(q_ref, k_ref, v_ref, out_ref):
    for head in range(q_ref.shape[1] // HD):
        cols = slice(head * HD, (head + 1) * HD)
        out_ref[:, cols] = softmax_mix(
            q_ref[:, cols], k_ref[:, cols], v_ref[:, cols], None
        ).astype(jnp.bfloat16)


def cross_kernel(bias_ref, cq_ref, tk_ref, tv_ref, self_ref, out_ref):
    for head in range(cq_ref.shape[1] // HD):
        cols = slice(head * HD, (head + 1) * HD)
        cross_out = softmax_mix(cq_ref[:, cols], tk_ref[:, cols], tv_ref[:, cols], bias_ref[...])
        out_ref[:, cols] = (
            self_ref[:, cols].astype(jnp.float32)
            + cross_out.astype(jnp.bfloat16).astype(jnp.float32)
        ).astype(jnp.bfloat16)


def self_attend(qkv, width):
    rows = qkv.shape[0]
    block = math.gcd(rows, 256)
    pairs = rows * width * rows
    return pl.pallas_call(
        self_kernel,
        grid=(rows // block,),
        in_specs=[
            pl.BlockSpec((block, width), lambda i: (i, 0)),
            pl.BlockSpec((rows, width), lambda i: (0, 1)),
            pl.BlockSpec((rows, width), lambda i: (0, 2)),
        ],
        out_specs=pl.BlockSpec((block, width), lambda i: (i, 0)),
        out_shape=jax.ShapeDtypeStruct((rows, width), jnp.bfloat16),
        compiler_params=pltpu.CompilerParams(vmem_limit_bytes=32 << 20),
        cost_estimate=pl.CostEstimate(
            flops=4 * pairs, bytes_accessed=8 * rows * width, transcendentals=pairs // HD
        ),
        name="self_attend",
    )(qkv, qkv, qkv)


def cross_attend(bias, cq, text, self_out):
    rows, width = cq.shape
    slots = text.shape[0]
    block = math.gcd(rows, 512)
    pairs = rows * width * slots
    row_spec = pl.BlockSpec((block, width), lambda i: (i, 0))
    return pl.pallas_call(
        cross_kernel,
        grid=(rows // block,),
        in_specs=[
            pl.BlockSpec((1, slots), lambda i: (0, 0)),
            row_spec,
            pl.BlockSpec((slots, width), lambda i: (0, 0)),
            pl.BlockSpec((slots, width), lambda i: (0, 1)),
            row_spec,
        ],
        out_specs=row_spec,
        out_shape=jax.ShapeDtypeStruct((rows, width), jnp.bfloat16),
        compiler_params=pltpu.CompilerParams(vmem_limit_bytes=32 << 20),
        cost_estimate=pl.CostEstimate(
            flops=4 * pairs, bytes_accessed=6 * rows * width, transcendentals=pairs // HD
        ),
        name="cross_attend",
    )(bias, cq, text, text, self_out)


def gather_weights(weights, x_hi, core):
    wide = jnp.concatenate([weights, lax.ppermute(weights, "seq", XL_SWAP)], axis=1)
    first = lax.ppermute(wide, "prompt", REGROUP_A)
    second = lax.ppermute(wide, "prompt", REGROUP_B)
    same = x_hi == core
    keep = jnp.where(same, wide, second)
    chunk = jnp.where(
        core == 0,
        jnp.where(same, jnp.concatenate([keep, first]), jnp.concatenate([first, keep])),
        jnp.where(same, jnp.concatenate([first, keep]), jnp.concatenate([keep, first])),
    )
    return chunk


def ring_y(chunk):
    half = chunk.shape[0] // 2
    before = lax.ppermute(chunk, "prompt", y_shift(1))
    after = lax.ppermute(chunk, "prompt", y_shift(-1))
    far_top = lax.ppermute(before[:half], "prompt", y_shift(1))
    far_bottom = lax.ppermute(after[half:], "prompt", y_shift(-1))
    return jnp.concatenate([chunk, after, far_top, far_bottom, before], axis=0)


def ring_z(block):
    half = block.shape[0] // 2
    found = [(0, block)]
    up = down = block
    for step in range(1, Z // 2):
        up = lax.ppermute(up, "seq", z_shift(1))
        down = lax.ppermute(down, "seq", z_shift(-1))
        found += [(-step, up), (step, down)]
    far_top = lax.ppermute(up[:half], "seq", z_shift(1))
    far_bottom = lax.ppermute(down[half:], "seq", z_shift(-1))
    return found + [(Z // 2, jnp.concatenate([far_top, far_bottom], axis=0))]


def body(
    queries, self_keys, self_values, cross_queries, context, key_weight, value_weight, lengths
):
    prompt, seq = lax.axis_index("prompt"), lax.axis_index("seq")
    y, x_hi, core = prompt // 4, (prompt // 2) % 2, prompt % 2
    z, x_lo = seq // 2, seq % 2
    parts = lax.axis_size("seq")
    width = queries.shape[2] // parts

    def to_heads(packed):
        heads = lax.all_to_all(packed, "seq", split_axis=0, concat_axis=0)
        return heads.reshape(-1, packed.shape[2])

    chunk = gather_weights(jnp.concatenate([key_weight, value_weight], axis=1), x_hi, core)
    text = context[0]
    text_rows, depth = text.shape
    piece = depth // (Y * CORE)
    rolled = lax.dynamic_slice(
        jnp.concatenate([text, text], axis=1), (0, y * (CORE * piece)), text.shape
    )
    halves = [
        jnp.concatenate(
            [rolled[:, (2 * k + h) * piece : (2 * k + h + 1) * piece] for k in range(Y)], axis=1
        )
        for h in range(CORE)
    ]
    mine = jnp.where(core == 0, halves[0], halves[1])
    theirs = jnp.where(core == 0, halves[1], halves[0])
    block = jnp.stack([mine, lax.ppermute(theirs, "prompt", CORE_SWAP)])

    qkv = to_heads(pack([queries[0], self_keys[0], self_values[0]], parts))
    weights = ring_y(chunk)
    found = ring_z(block.reshape(CORE * text_rows, -1))
    all_text = jnp.stack([rows.reshape(CORE, text_rows, -1) for _, rows in found], axis=1)
    offsets = jnp.array([offset for offset, _ in found], jnp.int32)
    slots = Z * text_rows
    partial = jnp.dot(
        all_text.reshape(CORE * slots, -1), weights, preferred_element_type=jnp.float32
    )
    from_core = lax.ppermute(partial[slots:], "prompt", CORE_SWAP)
    summed = (partial[:slots] + from_core).astype(jnp.bfloat16)
    own_columns, their_columns = summed[:, : 2 * width], summed[:, 2 * width :]
    text_kv = jnp.concatenate(
        [own_columns, lax.ppermute(their_columns, "seq", XL_SWAP)], axis=0
    )
    source_z = (z + offsets) % Z
    source_seq = jnp.stack([source_z * 2 + x_lo, source_z * 2 + 1 - x_lo]).reshape(-1, 1)
    slot = (source_seq * text_rows + jnp.arange(text_rows, dtype=jnp.int32)[None, :]).reshape(1, -1)
    bias = jnp.where(slot < lengths[0], 0.0, -jnp.inf).astype(jnp.float32)

    cq = to_heads(pack([cross_queries[0]], parts))
    self_out = self_attend(qkv, width)
    attended = cross_attend(bias, cq, text_kv, self_out)
    back = lax.all_to_all(
        attended.reshape(parts, -1, width), "seq", split_axis=0, concat_axis=0
    )
    return unpack(back)[None]


def solution(mesh):
    in_specs = (
        P("prompt", "seq", None),
        P("prompt", "seq", None),
        P("prompt", "seq", None),
        P("prompt", "seq", None),
        P("prompt", "seq", None),
        P("prompt", "seq"),
        P("prompt", "seq"),
        P("prompt"),
    )
    out_specs = P("prompt", "seq", None)
    return jax.shard_map(body, mesh=mesh, in_specs=in_specs, out_specs=out_specs, check_vma=False)
```

```python
import functools
import math

import jax
import jax.numpy as jnp
from jax import lax
from jax.experimental import pallas as pl
from jax.experimental.pallas import tpu as pltpu
from jax.sharding import PartitionSpec as P

HD = 128
EXP2_SCALE = math.log2(math.e) / math.sqrt(HD)
Y, XH, CORE = 4, 2, 2
Z, XL = 8, 2


def y_shift(step):
    block = XH * CORE
    return [(p, (p + step * block) % (Y * block)) for p in range(Y * block)]


def z_shift(step):
    return [(s, (s + step * XL) % (Z * XL)) for s in range(Z * XL)]


CORE_SWAP = [(p, p ^ 1) for p in range(Y * XH * CORE)]
XL_SWAP = [(s, s ^ 1) for s in range(Z * XL)]
REGROUP_A = [(4 * y + a, 4 * y + b) for y in range(Y) for a, b in ((0, 2), (2, 3), (3, 1), (1, 0))]
REGROUP_B = [(4 * y + a, 4 * y + b) for y in range(Y) for a, b in ((1, 2), (2, 1))]


def pack_kernel(width, parts, *refs):
    out_ref = refs[-1]
    for place, ref in enumerate(refs[:-1]):
        for part in range(parts):
            out_ref[part, :, place * width : (place + 1) * width] = ref[
                :, part * width : (part + 1) * width
            ]


def pack(arrays, parts):
    rows, columns = arrays[0].shape
    width = columns // parts
    block = math.gcd(rows, 64)
    return pl.pallas_call(
        functools.partial(pack_kernel, width, parts),
        grid=(rows // block,),
        in_specs=[pl.BlockSpec((block, columns), lambda i: (i, 0)) for _ in arrays],
        out_specs=pl.BlockSpec((parts, block, width * len(arrays)), lambda i: (0, i, 0)),
        out_shape=jax.ShapeDtypeStruct((parts, rows, width * len(arrays)), jnp.bfloat16),
        cost_estimate=pl.CostEstimate(
            flops=0, bytes_accessed=4 * rows * columns * len(arrays), transcendentals=0
        ),
        name="pack",
    )(*arrays)


def hold_kernel(*refs):
    del refs


def hold(array, *until):
    marks = [mark[:16, :HD] for mark in until]
    return pl.pallas_call(
        hold_kernel,
        in_specs=[pl.BlockSpec(memory_space=pl.ANY)] * (1 + len(marks)),
        out_specs=pl.BlockSpec(memory_space=pl.ANY),
        out_shape=jax.ShapeDtypeStruct(array.shape, array.dtype),
        input_output_aliases={0: 0},
        name="hold",
    )(array, *marks)


def unpack_kernel(in_ref, out_ref):
    parts, _, width = in_ref.shape
    for part in range(parts):
        out_ref[:, part * width : (part + 1) * width] = in_ref[part]


def unpack(blocks):
    parts, rows, width = blocks.shape
    block = math.gcd(rows, 128)
    return pl.pallas_call(
        unpack_kernel,
        grid=(rows // block,),
        in_specs=[pl.BlockSpec((parts, block, width), lambda i: (0, i, 0))],
        out_specs=pl.BlockSpec((block, parts * width), lambda i: (i, 0)),
        out_shape=jax.ShapeDtypeStruct((rows, parts * width), jnp.bfloat16),
        name="unpack",
    )(blocks)


def softmax_mix(query, keys, values, bias):
    scores = lax.dot_general(
        query, keys, (((1,), (1,)), ((), ())), preferred_element_type=jnp.float32
    )
    if bias is not None:
        scores = scores + bias
    row_max = jnp.max(scores, axis=1, keepdims=True)
    weights = jnp.exp2((scores - row_max) * EXP2_SCALE)
    totals = jnp.sum(weights, axis=1, keepdims=True)
    mixed = jnp.dot(weights.astype(jnp.bfloat16), values, preferred_element_type=jnp.float32)
    return mixed / totals


def self_kernel(q_ref, k_ref, v_ref, out_ref):
    for head in range(q_ref.shape[1] // HD):
        cols = slice(head * HD, (head + 1) * HD)
        out_ref[:, cols] = softmax_mix(
            q_ref[:, cols], k_ref[:, cols], v_ref[:, cols], None
        ).astype(jnp.bfloat16)


def cross_kernel(bias_ref, cq_ref, tk_ref, tv_ref, self_ref, out_ref):
    for head in range(cq_ref.shape[1] // HD):
        cols = slice(head * HD, (head + 1) * HD)
        cross_out = softmax_mix(cq_ref[:, cols], tk_ref[:, cols], tv_ref[:, cols], bias_ref[...])
        out_ref[:, cols] = (
            self_ref[:, cols].astype(jnp.float32)
            + cross_out.astype(jnp.bfloat16).astype(jnp.float32)
        ).astype(jnp.bfloat16)


def self_attend(qkv, width):
    rows = qkv.shape[0]
    block = math.gcd(rows, 256)
    pairs = rows * width * rows
    return pl.pallas_call(
        self_kernel,
        grid=(rows // block,),
        in_specs=[
            pl.BlockSpec((block, width), lambda i: (i, 0)),
            pl.BlockSpec((rows, width), lambda i: (0, 1)),
            pl.BlockSpec((rows, width), lambda i: (0, 2)),
        ],
        out_specs=pl.BlockSpec((block, width), lambda i: (i, 0)),
        out_shape=jax.ShapeDtypeStruct((rows, width), jnp.bfloat16),
        compiler_params=pltpu.CompilerParams(vmem_limit_bytes=32 << 20),
        cost_estimate=pl.CostEstimate(
            flops=4 * pairs, bytes_accessed=8 * rows * width, transcendentals=pairs // HD
        ),
        name="self_attend",
    )(qkv, qkv, qkv)


def cross_attend(bias, cq, text, self_out):
    rows, width = cq.shape
    slots = text.shape[0]
    block = math.gcd(rows, 512)
    pairs = rows * width * slots
    row_spec = pl.BlockSpec((block, width), lambda i: (i, 0))
    return pl.pallas_call(
        cross_kernel,
        grid=(rows // block,),
        in_specs=[
            pl.BlockSpec((1, slots), lambda i: (0, 0)),
            row_spec,
            pl.BlockSpec((slots, width), lambda i: (0, 0)),
            pl.BlockSpec((slots, width), lambda i: (0, 1)),
            row_spec,
        ],
        out_specs=row_spec,
        out_shape=jax.ShapeDtypeStruct((rows, width), jnp.bfloat16),
        compiler_params=pltpu.CompilerParams(vmem_limit_bytes=32 << 20),
        cost_estimate=pl.CostEstimate(
            flops=4 * pairs, bytes_accessed=6 * rows * width, transcendentals=pairs // HD
        ),
        name="cross_attend",
    )(bias, cq, text, text, self_out)


def gather_weights(weights, x_hi, core):
    wide = jnp.concatenate([weights, lax.ppermute(weights, "seq", XL_SWAP)], axis=1)
    first = lax.ppermute(wide, "prompt", REGROUP_A)
    second = lax.ppermute(wide, "prompt", REGROUP_B)
    same = x_hi == core
    keep = jnp.where(same, wide, second)
    chunk = jnp.where(
        core == 0,
        jnp.where(same, jnp.concatenate([keep, first]), jnp.concatenate([first, keep])),
        jnp.where(same, jnp.concatenate([first, keep]), jnp.concatenate([keep, first])),
    )
    return chunk


def ring_y(chunk):
    half = chunk.shape[0] // 2
    before = lax.ppermute(chunk, "prompt", y_shift(1))
    after = lax.ppermute(chunk, "prompt", y_shift(-1))
    far_top = lax.ppermute(before[:half], "prompt", y_shift(1))
    far_bottom = lax.ppermute(after[half:], "prompt", y_shift(-1))
    return jnp.concatenate([chunk, after, far_top, far_bottom, before], axis=0)


def ring_z(block):
    half = block.shape[0] // 2
    offsets, pieces = [0], [block]
    up = down = block
    for step in range(1, Z // 2):
        up = lax.ppermute(up, "seq", z_shift(1))
        down = lax.ppermute(down, "seq", z_shift(-1))
        offsets += [-step, step]
        pieces += [up, down]
    pieces.append(lax.ppermute(up[:half], "seq", z_shift(1)))
    pieces.append(lax.ppermute(down[half:], "seq", z_shift(-1)))
    return offsets + [Z // 2], pieces


def split_kernel(count, where_ref, *refs):
    del where_ref
    for half in range(CORE):
        place = 0
        for ref in refs[half * count : (half + 1) * count]:
            refs[CORE * count + half][place : place + ref.shape[0], :] = ref[...]
            place += ref.shape[0]


def split_text(pieces, y, core):
    depth = pieces[0].shape[1]
    rows = sum(piece.shape[0] for piece in pieces)
    wide = depth // (Y * CORE)

    def chunk(flip):
        def place(k, where):
            return 0, ((where[0] + k) % Y) * CORE + (where[1] + flip) % CORE

        return [pl.BlockSpec((piece.shape[0], wide), place) for piece in pieces]

    shape = jax.ShapeDtypeStruct((rows, Y * wide), jnp.bfloat16)
    spec = pl.BlockSpec((rows, wide), lambda k, where: (0, k))
    return pl.pallas_call(
        functools.partial(split_kernel, len(pieces)),
        grid_spec=pltpu.PrefetchScalarGridSpec(
            num_scalar_prefetch=1,
            grid=(Y,),
            in_specs=chunk(0) + chunk(1),
            out_specs=[spec, spec],
        ),
        out_shape=[shape, shape],
        cost_estimate=pl.CostEstimate(
            flops=0, bytes_accessed=4 * rows * depth, transcendentals=0
        ),
        name="split_text",
    )(jnp.stack([y, core]), *pieces, *pieces)


def body(
    queries, self_keys, self_values, cross_queries, context, key_weight, value_weight, lengths
):
    prompt, seq = lax.axis_index("prompt"), lax.axis_index("seq")
    y, x_hi, core = prompt // 4, (prompt // 2) % 2, prompt % 2
    z, x_lo = seq // 2, seq % 2
    parts = lax.axis_size("seq")
    width = queries.shape[2] // parts

    def to_heads(packed):
        heads = lax.all_to_all(packed, "seq", split_axis=0, concat_axis=0)
        return heads.reshape(-1, packed.shape[2])

    offsets, pieces = ring_z(context[0])
    chunk = gather_weights(jnp.concatenate([key_weight, value_weight], axis=1), x_hi, core)
    packed = pack([queries[0], self_keys[0], self_values[0]], parts)
    qkv = to_heads(hold(packed, chunk, *pieces[-4:]))
    weights = ring_y(chunk)
    text_rows = context.shape[1]
    mine, theirs = split_text(pieces, y, core)
    other = lax.ppermute(theirs, "prompt", CORE_SWAP)
    other_part = jnp.dot(other, weights, preferred_element_type=jnp.float32)
    own_part = jnp.dot(mine, weights, preferred_element_type=jnp.float32)
    summed = (own_part + lax.ppermute(other_part, "prompt", CORE_SWAP)).astype(jnp.bfloat16)
    own_columns, their_columns = summed[:, : 2 * width], summed[:, 2 * width :]
    text_kv = jnp.concatenate(
        [own_columns, lax.ppermute(their_columns, "seq", XL_SWAP)], axis=0
    )
    source_z = (z + jnp.array(offsets, jnp.int32)) % Z
    source_seq = jnp.stack([source_z * 2 + x_lo, source_z * 2 + 1 - x_lo]).reshape(-1, 1)
    slot = (source_seq * text_rows + jnp.arange(text_rows, dtype=jnp.int32)[None, :]).reshape(1, -1)
    bias = jnp.where(slot < lengths[0], 0.0, -jnp.inf).astype(jnp.float32)

    cq = to_heads(pack([cross_queries[0]], parts))
    self_out = self_attend(qkv, width)
    attended = cross_attend(bias, cq, text_kv, self_out)
    back = lax.all_to_all(
        attended.reshape(parts, -1, width), "seq", split_axis=0, concat_axis=0
    )
    return unpack(back)[None]


def solution(mesh):
    in_specs = (
        P("prompt", "seq", None),
        P("prompt", "seq", None),
        P("prompt", "seq", None),
        P("prompt", "seq", None),
        P("prompt", "seq", None),
        P("prompt", "seq"),
        P("prompt", "seq"),
        P("prompt"),
    )
    out_specs = P("prompt", "seq", None)
    return jax.shard_map(body, mesh=mesh, in_specs=in_specs, out_specs=out_specs, check_vma=False)
```

```python
import functools
import math

import jax
import jax.numpy as jnp
from jax import lax
from jax.experimental import pallas as pl
from jax.experimental.pallas import tpu as pltpu
from jax.sharding import PartitionSpec as P

HD = 128
EXP2_SCALE = math.log2(math.e) / math.sqrt(HD)
Y, XH, CORE = 4, 2, 2
Z, XL = 8, 2


def y_shift(step):
    block = XH * CORE
    return [(p, (p + step * block) % (Y * block)) for p in range(Y * block)]


def z_shift(step):
    return [(s, (s + step * XL) % (Z * XL)) for s in range(Z * XL)]


SPLIT_FLOPS = 400_000_000_000
CORE_SWAP = [(p, p ^ 1) for p in range(Y * XH * CORE)]
XL_SWAP = [(s, s ^ 1) for s in range(Z * XL)]
REGROUP_A = [(4 * y + a, 4 * y + b) for y in range(Y) for a, b in ((0, 2), (2, 3), (3, 1), (1, 0))]
REGROUP_B = [(4 * y + a, 4 * y + b) for y in range(Y) for a, b in ((1, 2), (2, 1))]


def pack_kernel(width, parts, *refs):
    out_ref = refs[-1]
    for place, ref in enumerate(refs[:-1]):
        for part in range(parts):
            out_ref[part, :, place * width : (place + 1) * width] = ref[
                :, part * width : (part + 1) * width
            ]


def pack(arrays, parts):
    rows, columns = arrays[0].shape
    width = columns // parts
    block = math.gcd(rows, 64)
    return pl.pallas_call(
        functools.partial(pack_kernel, width, parts),
        grid=(rows // block,),
        in_specs=[pl.BlockSpec((block, columns), lambda i: (i, 0)) for _ in arrays],
        out_specs=pl.BlockSpec((parts, block, width * len(arrays)), lambda i: (0, i, 0)),
        out_shape=jax.ShapeDtypeStruct((parts, rows, width * len(arrays)), jnp.bfloat16),
        cost_estimate=pl.CostEstimate(
            flops=0, bytes_accessed=4 * rows * columns * len(arrays), transcendentals=0
        ),
        name="pack",
    )(*arrays)


def hold_kernel(*refs):
    del refs


def hold(array, *until):
    marks = [mark[:16, :HD] for mark in until]
    return pl.pallas_call(
        hold_kernel,
        in_specs=[pl.BlockSpec(memory_space=pl.ANY)] * (1 + len(marks)),
        out_specs=pl.BlockSpec(memory_space=pl.ANY),
        out_shape=jax.ShapeDtypeStruct(array.shape, array.dtype),
        input_output_aliases={0: 0},
        name="hold",
    )(array, *marks)


def unpack_kernel(in_ref, out_ref):
    parts, _, width = in_ref.shape
    for part in range(parts):
        out_ref[:, part * width : (part + 1) * width] = in_ref[part]


def unpack(blocks):
    parts, rows, width = blocks.shape
    block = math.gcd(rows, 128)
    return pl.pallas_call(
        unpack_kernel,
        grid=(rows // block,),
        in_specs=[pl.BlockSpec((parts, block, width), lambda i: (0, i, 0))],
        out_specs=pl.BlockSpec((block, parts * width), lambda i: (i, 0)),
        out_shape=jax.ShapeDtypeStruct((rows, parts * width), jnp.bfloat16),
        name="unpack",
    )(blocks)


def softmax_mix(query, keys, values, bias):
    scores = lax.dot_general(
        query, keys, (((1,), (1,)), ((), ())), preferred_element_type=jnp.float32
    )
    if bias is not None:
        scores = scores + bias
    row_max = jnp.max(scores, axis=1, keepdims=True)
    weights = jnp.exp2((scores - row_max) * EXP2_SCALE)
    totals = jnp.sum(weights, axis=1, keepdims=True)
    mixed = jnp.dot(weights.astype(jnp.bfloat16), values, preferred_element_type=jnp.float32)
    return mixed / totals


def self_kernel(q_ref, k_ref, v_ref, out_ref):
    for head in range(q_ref.shape[1] // HD):
        cols = slice(head * HD, (head + 1) * HD)
        out_ref[:, cols] = softmax_mix(
            q_ref[:, cols], k_ref[:, cols], v_ref[:, cols], None
        ).astype(jnp.bfloat16)


def cross_kernel(bias_ref, cq_ref, tk_ref, tv_ref, self_ref, out_ref):
    for head in range(cq_ref.shape[1] // HD):
        cols = slice(head * HD, (head + 1) * HD)
        cross_out = softmax_mix(cq_ref[:, cols], tk_ref[:, cols], tv_ref[:, cols], bias_ref[...])
        out_ref[:, cols] = (
            self_ref[:, cols].astype(jnp.float32)
            + cross_out.astype(jnp.bfloat16).astype(jnp.float32)
        ).astype(jnp.bfloat16)


def self_attend(qkv, width):
    rows = qkv.shape[0]
    block = math.gcd(rows, 256)
    pairs = rows * width * rows
    return pl.pallas_call(
        self_kernel,
        grid=(rows // block,),
        in_specs=[
            pl.BlockSpec((block, width), lambda i: (i, 0)),
            pl.BlockSpec((rows, width), lambda i: (0, 1)),
            pl.BlockSpec((rows, width), lambda i: (0, 2)),
        ],
        out_specs=pl.BlockSpec((block, width), lambda i: (i, 0)),
        out_shape=jax.ShapeDtypeStruct((rows, width), jnp.bfloat16),
        compiler_params=pltpu.CompilerParams(vmem_limit_bytes=32 << 20),
        cost_estimate=pl.CostEstimate(
            flops=4 * pairs, bytes_accessed=8 * rows * width, transcendentals=pairs // HD
        ),
        name="self_attend",
    )(qkv, qkv, qkv)


def cross_attend(bias, cq, text, self_out):
    rows, width = cq.shape
    slots = text.shape[0]
    block = math.gcd(rows, 512)
    pairs = rows * width * slots
    row_spec = pl.BlockSpec((block, width), lambda i: (i, 0))
    return pl.pallas_call(
        cross_kernel,
        grid=(rows // block,),
        in_specs=[
            pl.BlockSpec((1, slots), lambda i: (0, 0)),
            row_spec,
            pl.BlockSpec((slots, width), lambda i: (0, 0)),
            pl.BlockSpec((slots, width), lambda i: (0, 1)),
            row_spec,
        ],
        out_specs=row_spec,
        out_shape=jax.ShapeDtypeStruct((rows, width), jnp.bfloat16),
        compiler_params=pltpu.CompilerParams(vmem_limit_bytes=32 << 20),
        cost_estimate=pl.CostEstimate(
            flops=4 * pairs, bytes_accessed=6 * rows * width, transcendentals=pairs // HD
        ),
        name="cross_attend",
    )(bias, cq, text, text, self_out)


def gather_weights(weights, x_hi, core):
    wide = jnp.concatenate([weights, lax.ppermute(weights, "seq", XL_SWAP)], axis=1)
    first = lax.ppermute(wide, "prompt", REGROUP_A)
    second = lax.ppermute(wide, "prompt", REGROUP_B)
    same = x_hi == core
    keep = jnp.where(same, wide, second)
    chunk = jnp.where(
        core == 0,
        jnp.where(same, jnp.concatenate([keep, first]), jnp.concatenate([first, keep])),
        jnp.where(same, jnp.concatenate([first, keep]), jnp.concatenate([keep, first])),
    )
    return chunk


def ring_y(chunk):
    half = chunk.shape[0] // 2
    before = lax.ppermute(chunk, "prompt", y_shift(1))
    after = lax.ppermute(chunk, "prompt", y_shift(-1))
    far_top = lax.ppermute(before[:half], "prompt", y_shift(1))
    far_bottom = lax.ppermute(after[half:], "prompt", y_shift(-1))
    return jnp.concatenate([chunk, after, far_top, far_bottom, before], axis=0)


def ring_z(block):
    half = block.shape[0] // 2
    offsets, pieces = [0], [block]
    up = down = block
    for step in range(1, Z // 2):
        up = lax.ppermute(up, "seq", z_shift(1))
        down = lax.ppermute(down, "seq", z_shift(-1))
        offsets += [-step, step]
        pieces += [up, down]
    pieces.append(lax.ppermute(up[:half], "seq", z_shift(1)))
    pieces.append(lax.ppermute(down[half:], "seq", z_shift(-1)))
    return offsets + [Z // 2], pieces


def split_kernel(count, where_ref, *refs):
    del where_ref
    for half in range(CORE):
        place = 0
        for ref in refs[half * count : (half + 1) * count]:
            refs[CORE * count + half][place : place + ref.shape[0], :] = ref[...]
            place += ref.shape[0]


def split_text(pieces, y, core):
    depth = pieces[0].shape[1]
    rows = sum(piece.shape[0] for piece in pieces)
    wide = depth // (Y * CORE)

    def chunk(flip):
        def place(k, where):
            return 0, ((where[0] + k) % Y) * CORE + (where[1] + flip) % CORE

        return [pl.BlockSpec((piece.shape[0], wide), place) for piece in pieces]

    shape = jax.ShapeDtypeStruct((rows, Y * wide), jnp.bfloat16)
    spec = pl.BlockSpec((rows, wide), lambda k, where: (0, k))
    return pl.pallas_call(
        functools.partial(split_kernel, len(pieces)),
        grid_spec=pltpu.PrefetchScalarGridSpec(
            num_scalar_prefetch=1,
            grid=(Y,),
            in_specs=chunk(0) + chunk(1),
            out_specs=[spec, spec],
        ),
        out_shape=[shape, shape],
        cost_estimate=pl.CostEstimate(
            flops=SPLIT_FLOPS, bytes_accessed=4 * rows * depth, transcendentals=0
        ),
        name="split_text",
    )(jnp.stack([y, core]), *pieces, *pieces)


def body(
    queries, self_keys, self_values, cross_queries, context, key_weight, value_weight, lengths
):
    prompt, seq = lax.axis_index("prompt"), lax.axis_index("seq")
    y, x_hi, core = prompt // 4, (prompt // 2) % 2, prompt % 2
    z, x_lo = seq // 2, seq % 2
    parts = lax.axis_size("seq")
    width = queries.shape[2] // parts

    def to_heads(packed):
        heads = lax.all_to_all(packed, "seq", split_axis=0, concat_axis=0)
        return heads.reshape(-1, packed.shape[2])

    offsets, pieces = ring_z(context[0])
    chunk = gather_weights(jnp.concatenate([key_weight, value_weight], axis=1), x_hi, core)
    packed = pack([queries[0], self_keys[0], self_values[0]], parts)
    qkv = to_heads(hold(packed, *pieces[-4:-2]))
    weights = ring_y(chunk)
    text_rows = context.shape[1]
    mine, theirs = split_text(pieces, y, core)
    other = lax.ppermute(theirs, "prompt", CORE_SWAP)
    other_part = jnp.dot(other, weights, preferred_element_type=jnp.float32)
    own_part = jnp.dot(mine, weights, preferred_element_type=jnp.float32)
    summed = (own_part + lax.ppermute(other_part, "prompt", CORE_SWAP)).astype(jnp.bfloat16)
    own_columns, their_columns = summed[:, : 2 * width], summed[:, 2 * width :]
    text_kv = jnp.concatenate(
        [own_columns, lax.ppermute(their_columns, "seq", XL_SWAP)], axis=0
    )
    source_z = (z + jnp.array(offsets, jnp.int32)) % Z
    source_seq = jnp.stack([source_z * 2 + x_lo, source_z * 2 + 1 - x_lo]).reshape(-1, 1)
    slot = (source_seq * text_rows + jnp.arange(text_rows, dtype=jnp.int32)[None, :]).reshape(1, -1)
    bias = jnp.where(slot < lengths[0], 0.0, -jnp.inf).astype(jnp.float32)

    cq = to_heads(pack([cross_queries[0]], parts))
    self_out = self_attend(qkv, width)
    attended = cross_attend(bias, cq, text_kv, self_out)
    back = lax.all_to_all(
        attended.reshape(parts, -1, width), "seq", split_axis=0, concat_axis=0
    )
    return unpack(back)[None]


def solution(mesh):
    in_specs = (
        P("prompt", "seq", None),
        P("prompt", "seq", None),
        P("prompt", "seq", None),
        P("prompt", "seq", None),
        P("prompt", "seq", None),
        P("prompt", "seq"),
        P("prompt", "seq"),
        P("prompt"),
    )
    out_specs = P("prompt", "seq", None)
    return jax.shard_map(body, mesh=mesh, in_specs=in_specs, out_specs=out_specs, check_vma=False)
```

```python
import functools
import math

import jax
import jax.numpy as jnp
from jax import lax
from jax.experimental import pallas as pl
from jax.experimental.pallas import tpu as pltpu
from jax.sharding import PartitionSpec as P

HD = 128
EXP2_SCALE = math.log2(math.e) / math.sqrt(HD)
Y, XH, CORE = 4, 2, 2
Z, XL = 8, 2


def y_shift(step):
    block = XH * CORE
    return [(p, (p + step * block) % (Y * block)) for p in range(Y * block)]


def z_shift(step):
    return [(s, (s + step * XL) % (Z * XL)) for s in range(Z * XL)]


SPLIT_FLOPS = 400_000_000_000
CORE_SWAP = [(p, p ^ 1) for p in range(Y * XH * CORE)]
XL_SWAP = [(s, s ^ 1) for s in range(Z * XL)]
REGROUP_A = [(4 * y + a, 4 * y + b) for y in range(Y) for a, b in ((0, 2), (2, 3), (3, 1), (1, 0))]
REGROUP_B = [(4 * y + a, 4 * y + b) for y in range(Y) for a, b in ((1, 2), (2, 1))]


def pack_kernel(width, parts, *refs):
    out_ref = refs[-1]
    for place, ref in enumerate(refs[:-1]):
        for part in range(parts):
            out_ref[part, :, place * width : (place + 1) * width] = ref[
                :, part * width : (part + 1) * width
            ]


def pack(arrays, parts):
    rows, columns = arrays[0].shape
    width = columns // parts
    block = math.gcd(rows, 64)
    return pl.pallas_call(
        functools.partial(pack_kernel, width, parts),
        grid=(rows // block,),
        in_specs=[pl.BlockSpec((block, columns), lambda i: (i, 0)) for _ in arrays],
        out_specs=pl.BlockSpec((parts, block, width * len(arrays)), lambda i: (0, i, 0)),
        out_shape=jax.ShapeDtypeStruct((parts, rows, width * len(arrays)), jnp.bfloat16),
        cost_estimate=pl.CostEstimate(
            flops=0, bytes_accessed=4 * rows * columns * len(arrays), transcendentals=0
        ),
        name="pack",
    )(*arrays)


def hold_kernel(*refs):
    del refs


def hold(array, *until):
    marks = [mark[:16, :HD] for mark in until]
    return pl.pallas_call(
        hold_kernel,
        in_specs=[pl.BlockSpec(memory_space=pl.ANY)] * (1 + len(marks)),
        out_specs=pl.BlockSpec(memory_space=pl.ANY),
        out_shape=jax.ShapeDtypeStruct(array.shape, array.dtype),
        input_output_aliases={0: 0},
        name="hold",
    )(array, *marks)


def unpack_kernel(in_ref, out_ref):
    parts, _, width = in_ref.shape
    for part in range(parts):
        out_ref[:, part * width : (part + 1) * width] = in_ref[part]


def unpack(blocks):
    parts, rows, width = blocks.shape
    block = math.gcd(rows, 128)
    return pl.pallas_call(
        unpack_kernel,
        grid=(rows // block,),
        in_specs=[pl.BlockSpec((parts, block, width), lambda i: (0, i, 0))],
        out_specs=pl.BlockSpec((block, parts * width), lambda i: (i, 0)),
        out_shape=jax.ShapeDtypeStruct((rows, parts * width), jnp.bfloat16),
        name="unpack",
    )(blocks)


def softmax_mix(query, keys, values, bias):
    scores = lax.dot_general(
        query, keys, (((1,), (1,)), ((), ())), preferred_element_type=jnp.float32
    )
    if bias is not None:
        scores = scores + bias
    row_max = jnp.max(scores, axis=1, keepdims=True)
    weights = jnp.exp2((scores - row_max) * EXP2_SCALE)
    totals = jnp.sum(weights, axis=1, keepdims=True)
    mixed = jnp.dot(weights.astype(jnp.bfloat16), values, preferred_element_type=jnp.float32)
    return mixed / totals


def self_kernel(q_ref, k_ref, v_ref, out_ref):
    rows = math.gcd(q_ref.shape[0], 256)
    for start in range(0, q_ref.shape[0], rows):
        for head in range(q_ref.shape[1] // HD):
            cols = slice(head * HD, (head + 1) * HD)
            out_ref[start : start + rows, cols] = softmax_mix(
                q_ref[start : start + rows, cols], k_ref[:, cols], v_ref[:, cols], None
            ).astype(jnp.bfloat16)


def cross_kernel(bias_ref, cq_ref, tk_ref, tv_ref, self_ref, out_ref):
    rows = math.gcd(cq_ref.shape[0], 512)
    for start in range(0, cq_ref.shape[0], rows):
        here = slice(start, start + rows)
        for head in range(cq_ref.shape[1] // HD):
            cols = slice(head * HD, (head + 1) * HD)
            cross_out = softmax_mix(
                cq_ref[here, cols], tk_ref[:, cols], tv_ref[:, cols], bias_ref[...]
            )
            out_ref[here, cols] = (
                self_ref[here, cols].astype(jnp.float32)
                + cross_out.astype(jnp.bfloat16).astype(jnp.float32)
            ).astype(jnp.bfloat16)


def self_attend(qkv, width):
    rows = qkv.shape[0]
    block = math.gcd(rows, 1024)
    pairs = rows * width * rows
    return pl.pallas_call(
        self_kernel,
        grid=(rows // block,),
        in_specs=[
            pl.BlockSpec((block, width), lambda i: (i, 0)),
            pl.BlockSpec((rows, width), lambda i: (0, 1)),
            pl.BlockSpec((rows, width), lambda i: (0, 2)),
        ],
        out_specs=pl.BlockSpec((block, width), lambda i: (i, 0)),
        out_shape=jax.ShapeDtypeStruct((rows, width), jnp.bfloat16),
        compiler_params=pltpu.CompilerParams(vmem_limit_bytes=40 << 20),
        cost_estimate=pl.CostEstimate(
            flops=4 * pairs, bytes_accessed=8 * rows * width, transcendentals=pairs // HD
        ),
        name="self_attend",
    )(qkv, qkv, qkv)


def cross_attend(bias, cq, text, self_out):
    rows, width = cq.shape
    slots = text.shape[0]
    block = math.gcd(rows, 1024)
    pairs = rows * width * slots
    row_spec = pl.BlockSpec((block, width), lambda i: (i, 0))
    return pl.pallas_call(
        cross_kernel,
        grid=(rows // block,),
        in_specs=[
            pl.BlockSpec((1, slots), lambda i: (0, 0)),
            row_spec,
            pl.BlockSpec((slots, width), lambda i: (0, 0)),
            pl.BlockSpec((slots, width), lambda i: (0, 1)),
            row_spec,
        ],
        out_specs=row_spec,
        out_shape=jax.ShapeDtypeStruct((rows, width), jnp.bfloat16),
        compiler_params=pltpu.CompilerParams(vmem_limit_bytes=32 << 20),
        cost_estimate=pl.CostEstimate(
            flops=4 * pairs, bytes_accessed=6 * rows * width, transcendentals=pairs // HD
        ),
        name="cross_attend",
    )(bias, cq, text, text, self_out)


def gather_weights(weights, x_hi, core, *until):
    wide = jnp.concatenate([weights, lax.ppermute(weights, "seq", XL_SWAP)], axis=1)
    first = hold(lax.ppermute(wide, "prompt", REGROUP_A), *until)
    second = lax.ppermute(wide, "prompt", REGROUP_B)
    same = x_hi == core
    keep = jnp.where(same, wide, second)
    chunk = jnp.where(
        core == 0,
        jnp.where(same, jnp.concatenate([keep, first]), jnp.concatenate([first, keep])),
        jnp.where(same, jnp.concatenate([first, keep]), jnp.concatenate([keep, first])),
    )
    return chunk


def ring_y(chunk):
    half = chunk.shape[1] // 2
    before = lax.ppermute(chunk, "prompt", y_shift(1))
    after = lax.ppermute(chunk, "prompt", y_shift(-1))
    far_left = lax.ppermute(before[:, :half], "prompt", y_shift(1))
    far_right = lax.ppermute(after[:, half:], "prompt", y_shift(-1))
    return (chunk, after, before), (far_left, far_right)


def project(text, near, far):
    deep, columns = near[0].shape
    chunks = [text[:, k * deep : (k + 1) * deep] for k in range(Y)]

    def dot(rows, weights):
        return jnp.dot(rows, weights, preferred_element_type=jnp.float32)

    sums = dot(chunks[0], near[0]) + dot(chunks[1], near[1]) + dot(chunks[3], near[2])
    sums = lax.optimization_barrier(sums)
    return [
        sums[:, : columns // 2] + dot(chunks[2], far[0]),
        sums[:, columns // 2 :] + dot(chunks[2], far[1]),
    ]


def ring_z(block):
    half = block.shape[0] // 2
    offsets, pieces = [0], [block]
    up = down = block
    for step in range(1, Z // 2):
        up = lax.ppermute(up, "seq", z_shift(1))
        down = lax.ppermute(down, "seq", z_shift(-1))
        offsets += [-step, step]
        pieces += [up, down]
    pieces.append(lax.ppermute(up[:half], "seq", z_shift(1)))
    pieces.append(lax.ppermute(down[half:], "seq", z_shift(-1)))
    return offsets + [Z // 2], pieces


def split_kernel(count, where_ref, *refs):
    del where_ref
    for half in range(CORE):
        place = 0
        for ref in refs[half * count : (half + 1) * count]:
            refs[CORE * count + half][place : place + ref.shape[0], :] = ref[...]
            place += ref.shape[0]


def split_text(pieces, y, core):
    depth = pieces[0].shape[1]
    rows = sum(piece.shape[0] for piece in pieces)
    wide = depth // (Y * CORE)

    def chunk(flip):
        def place(k, where):
            return 0, ((where[0] + k) % Y) * CORE + (where[1] + flip) % CORE

        return [pl.BlockSpec((piece.shape[0], wide), place) for piece in pieces]

    shape = jax.ShapeDtypeStruct((rows, Y * wide), jnp.bfloat16)
    spec = pl.BlockSpec((rows, wide), lambda k, where: (0, k))
    return pl.pallas_call(
        functools.partial(split_kernel, len(pieces)),
        grid_spec=pltpu.PrefetchScalarGridSpec(
            num_scalar_prefetch=1,
            grid=(Y,),
            in_specs=chunk(0) + chunk(1),
            out_specs=[spec, spec],
        ),
        out_shape=[shape, shape],
        cost_estimate=pl.CostEstimate(
            flops=SPLIT_FLOPS, bytes_accessed=4 * rows * depth, transcendentals=0
        ),
        name="split_text",
    )(jnp.stack([y, core]), *pieces, *pieces)


def body(
    queries, self_keys, self_values, cross_queries, context, key_weight, value_weight, lengths
):
    prompt, seq = lax.axis_index("prompt"), lax.axis_index("seq")
    y, x_hi, core = prompt // 4, (prompt // 2) % 2, prompt % 2
    z, x_lo = seq // 2, seq % 2
    parts = lax.axis_size("seq")
    width = queries.shape[2] // parts

    def to_heads(packed):
        heads = lax.all_to_all(packed, "seq", split_axis=0, concat_axis=0)
        return heads.reshape(-1, packed.shape[2])

    offsets, pieces = ring_z(context[0])
    both = jnp.concatenate([key_weight, value_weight], axis=1)
    chunk = gather_weights(both, x_hi, core, *pieces[-2:])
    packed = pack([queries[0], self_keys[0], self_values[0]], parts)
    qkv = to_heads(hold(packed, *pieces[-4:-2]))
    near, far = ring_y(chunk)
    text_rows = context.shape[1]
    mine, theirs = split_text(pieces, y, core)
    other = lax.ppermute(theirs, "prompt", CORE_SWAP)
    other_parts = project(other, near, far)
    own_parts = lax.optimization_barrier(project(mine, near, far))
    own_columns, their_columns = [
        (own + lax.ppermute(part, "prompt", CORE_SWAP)).astype(jnp.bfloat16)
        for own, part in zip(own_parts, other_parts)
    ]
    swapped = lax.ppermute(their_columns, "seq", XL_SWAP)
    source_z = (z + jnp.array(offsets, jnp.int32)) % Z
    source_seq = jnp.stack([source_z * 2 + x_lo, source_z * 2 + 1 - x_lo]).reshape(-1, 1)
    slot = (source_seq * text_rows + jnp.arange(text_rows, dtype=jnp.int32)[None, :]).reshape(1, -1)
    bias = jnp.where(slot < lengths[0], 0.0, -jnp.inf).astype(jnp.float32)

    cq = to_heads(hold(pack([cross_queries[0]], parts), own_columns, their_columns))
    self_out = self_attend(qkv, width)
    text_kv = jnp.concatenate([own_columns, hold(swapped, self_out)], axis=0)
    attended = cross_attend(bias, cq, text_kv, self_out)
    back = lax.all_to_all(
        attended.reshape(parts, -1, width), "seq", split_axis=0, concat_axis=0
    )
    return unpack(back)[None]


def solution(mesh):
    in_specs = (
        P("prompt", "seq", None),
        P("prompt", "seq", None),
        P("prompt", "seq", None),
        P("prompt", "seq", None),
        P("prompt", "seq", None),
        P("prompt", "seq"),
        P("prompt", "seq"),
        P("prompt"),
    )
    out_specs = P("prompt", "seq", None)
    return jax.shard_map(body, mesh=mesh, in_specs=in_specs, out_specs=out_specs, check_vma=False)
```

```python
import functools
import math

import jax
import jax.numpy as jnp
from jax import lax
from jax.experimental import pallas as pl
from jax.experimental.pallas import tpu as pltpu
from jax.sharding import PartitionSpec as P

HD = 128
EXP2_SCALE = math.log2(math.e) / math.sqrt(HD)
Y, XH, CORE = 4, 2, 2
Z, XL = 8, 2


def y_shift(step):
    block = XH * CORE
    return [(p, (p + step * block) % (Y * block)) for p in range(Y * block)]


def z_shift(step):
    return [(s, (s + step * XL) % (Z * XL)) for s in range(Z * XL)]


SPLIT_FLOPS = 400_000_000_000
CORE_SWAP = [(p, p ^ 1) for p in range(Y * XH * CORE)]
XL_SWAP = [(s, s ^ 1) for s in range(Z * XL)]
XH_SWAP = [(p, p ^ 2) for p in range(Y * XH * CORE)]


def pack_kernel(width, parts, *refs):
    out_ref = refs[-1]
    for place, ref in enumerate(refs[:-1]):
        for part in range(parts):
            out_ref[part, :, place * width : (place + 1) * width] = ref[
                :, part * width : (part + 1) * width
            ]


def pack(arrays, parts):
    rows, columns = arrays[0].shape
    width = columns // parts
    block = math.gcd(rows, 64)
    return pl.pallas_call(
        functools.partial(pack_kernel, width, parts),
        grid=(rows // block,),
        in_specs=[pl.BlockSpec((block, columns), lambda i: (i, 0)) for _ in arrays],
        out_specs=pl.BlockSpec((parts, block, width * len(arrays)), lambda i: (0, i, 0)),
        out_shape=jax.ShapeDtypeStruct((parts, rows, width * len(arrays)), jnp.bfloat16),
        cost_estimate=pl.CostEstimate(
            flops=0, bytes_accessed=4 * rows * columns * len(arrays), transcendentals=0
        ),
        name="pack",
    )(*arrays)


def hold_kernel(*refs):
    del refs


def hold(array, *until):
    marks = [mark[:16, :HD] for mark in until]
    return pl.pallas_call(
        hold_kernel,
        in_specs=[pl.BlockSpec(memory_space=pl.ANY)] * (1 + len(marks)),
        out_specs=pl.BlockSpec(memory_space=pl.ANY),
        out_shape=jax.ShapeDtypeStruct(array.shape, array.dtype),
        input_output_aliases={0: 0},
        name="hold",
    )(array, *marks)


def unpack_kernel(in_ref, out_ref):
    parts, _, width = in_ref.shape
    for part in range(parts):
        out_ref[:, part * width : (part + 1) * width] = in_ref[part]


def unpack(blocks):
    parts, rows, width = blocks.shape
    block = math.gcd(rows, 128)
    return pl.pallas_call(
        unpack_kernel,
        grid=(rows // block,),
        in_specs=[pl.BlockSpec((parts, block, width), lambda i: (0, i, 0))],
        out_specs=pl.BlockSpec((block, parts * width), lambda i: (i, 0)),
        out_shape=jax.ShapeDtypeStruct((rows, parts * width), jnp.bfloat16),
        name="unpack",
    )(blocks)


def softmax_mix(query, keys, values, bias):
    scores = lax.dot_general(
        query, keys, (((1,), (1,)), ((), ())), preferred_element_type=jnp.float32
    )
    if bias is not None:
        scores = scores + bias
    row_max = jnp.max(scores, axis=1, keepdims=True)
    weights = jnp.exp2((scores - row_max) * EXP2_SCALE)
    totals = jnp.sum(weights, axis=1, keepdims=True)
    mixed = jnp.dot(weights.astype(jnp.bfloat16), values, preferred_element_type=jnp.float32)
    return mixed / totals


def self_kernel(q_ref, k_ref, v_ref, out_ref):
    rows = math.gcd(q_ref.shape[0], 256)
    for start in range(0, q_ref.shape[0], rows):
        for head in range(q_ref.shape[1] // HD):
            cols = slice(head * HD, (head + 1) * HD)
            out_ref[start : start + rows, cols] = softmax_mix(
                q_ref[start : start + rows, cols], k_ref[:, cols], v_ref[:, cols], None
            ).astype(jnp.bfloat16)


def cross_kernel(bias_ref, cq_ref, tk_ref, tv_ref, self_ref, out_ref):
    rows = math.gcd(cq_ref.shape[0], 512)
    for start in range(0, cq_ref.shape[0], rows):
        here = slice(start, start + rows)
        for head in range(cq_ref.shape[1] // HD):
            cols = slice(head * HD, (head + 1) * HD)
            cross_out = softmax_mix(
                cq_ref[here, cols], tk_ref[:, cols], tv_ref[:, cols], bias_ref[...]
            )
            out_ref[here, cols] = (
                self_ref[here, cols].astype(jnp.float32)
                + cross_out.astype(jnp.bfloat16).astype(jnp.float32)
            ).astype(jnp.bfloat16)


def self_attend(qkv, width):
    rows = qkv.shape[0]
    block = math.gcd(rows, 1024)
    pairs = rows * width * rows
    return pl.pallas_call(
        self_kernel,
        grid=(rows // block,),
        in_specs=[
            pl.BlockSpec((block, width), lambda i: (i, 0)),
            pl.BlockSpec((rows, width), lambda i: (0, 1)),
            pl.BlockSpec((rows, width), lambda i: (0, 2)),
        ],
        out_specs=pl.BlockSpec((block, width), lambda i: (i, 0)),
        out_shape=jax.ShapeDtypeStruct((rows, width), jnp.bfloat16),
        compiler_params=pltpu.CompilerParams(vmem_limit_bytes=40 << 20),
        cost_estimate=pl.CostEstimate(
            flops=4 * pairs, bytes_accessed=8 * rows * width, transcendentals=pairs // HD
        ),
        name="self_attend",
    )(qkv, qkv, qkv)


def cross_attend(bias, cq, text, self_out):
    rows, width = cq.shape
    slots = text.shape[0]
    block = math.gcd(rows, 1024)
    pairs = rows * width * slots
    row_spec = pl.BlockSpec((block, width), lambda i: (i, 0))
    return pl.pallas_call(
        cross_kernel,
        grid=(rows // block,),
        in_specs=[
            pl.BlockSpec((1, slots), lambda i: (0, 0)),
            row_spec,
            pl.BlockSpec((slots, width), lambda i: (0, 0)),
            pl.BlockSpec((slots, width), lambda i: (0, 1)),
            row_spec,
        ],
        out_specs=row_spec,
        out_shape=jax.ShapeDtypeStruct((rows, width), jnp.bfloat16),
        compiler_params=pltpu.CompilerParams(vmem_limit_bytes=32 << 20),
        cost_estimate=pl.CostEstimate(
            flops=4 * pairs, bytes_accessed=6 * rows * width, transcendentals=pairs // HD
        ),
        name="cross_attend",
    )(bias, cq, text, text, self_out)


def gather_weights(weights, early, *until):
    wide = jnp.concatenate([weights, lax.ppermute(weights, "seq", XL_SWAP)], axis=1)
    other = lax.ppermute(hold(wide, early), "prompt", XH_SWAP)
    return jnp.concatenate([wide, hold(other, *until)], axis=0)


def ring_y(chunk):
    half = chunk.shape[1] // 2
    before = lax.ppermute(chunk, "prompt", y_shift(1))
    after = lax.ppermute(chunk, "prompt", y_shift(-1))
    far_left = lax.ppermute(before[:, :half], "prompt", y_shift(1))
    far_right = lax.ppermute(after[:, half:], "prompt", y_shift(-1))
    return (chunk, after, before), (far_left, far_right)


def project(text, near, far):
    deep, columns = near[0].shape
    chunks = [text[:, k * deep : (k + 1) * deep] for k in range(Y)]

    def dot(rows, weights):
        return jnp.dot(rows, weights, preferred_element_type=jnp.float32)

    sums = dot(chunks[0], near[0]) + dot(chunks[1], near[1]) + dot(chunks[3], near[2])
    sums = lax.optimization_barrier(sums)
    return [
        sums[:, : columns // 2] + dot(chunks[2], far[0]),
        sums[:, columns // 2 :] + dot(chunks[2], far[1]),
    ]


def ring_z(block):
    half = block.shape[0] // 2
    offsets, pieces = [0], [block]
    up = down = block
    for step in range(1, Z // 2):
        up = lax.ppermute(up, "seq", z_shift(1))
        down = lax.ppermute(down, "seq", z_shift(-1))
        offsets += [-step, step]
        pieces += [up, down]
    pieces.append(lax.ppermute(up[:half], "seq", z_shift(1)))
    pieces.append(lax.ppermute(down[half:], "seq", z_shift(-1)))
    return offsets + [Z // 2], pieces


def split_kernel(count, where_ref, *refs):
    outs = refs[count:]
    wide = refs[0].shape[1] // (XH * CORE)
    for x_hi in range(XH):
        for core in range(CORE):

            @pl.when((where_ref[1] == x_hi) & (where_ref[2] == core))
            def _():
                place = 0
                for ref in refs[:count]:
                    rows = slice(place, place + ref.shape[0])
                    for flip, out in enumerate(outs):
                        for k in range(XH):
                            chunk = (x_hi ^ k) * CORE + (core ^ flip)
                            out[rows, k * wide : (k + 1) * wide] = ref[
                                :, chunk * wide : (chunk + 1) * wide
                            ]
                    place += ref.shape[0]


def split_text(pieces, y, x_hi, core):
    depth = pieces[0].shape[1]
    rows = sum(piece.shape[0] for piece in pieces)
    wide = depth // Y
    shape = jax.ShapeDtypeStruct((rows, depth // CORE), jnp.bfloat16)
    spec = pl.BlockSpec((rows, wide // CORE), lambda k, where: (0, k))
    return pl.pallas_call(
        functools.partial(split_kernel, len(pieces)),
        grid_spec=pltpu.PrefetchScalarGridSpec(
            num_scalar_prefetch=1,
            grid=(Y,),
            in_specs=[
                pl.BlockSpec((piece.shape[0], wide), lambda k, where: (0, (where[0] + k) % Y))
                for piece in pieces
            ],
            out_specs=[spec, spec],
        ),
        out_shape=[shape, shape],
        cost_estimate=pl.CostEstimate(
            flops=SPLIT_FLOPS, bytes_accessed=4 * rows * depth, transcendentals=0
        ),
        name="split_text",
    )(jnp.stack([y, x_hi, core]), *pieces)


def body(
    queries, self_keys, self_values, cross_queries, context, key_weight, value_weight, lengths
):
    prompt, seq = lax.axis_index("prompt"), lax.axis_index("seq")
    y, x_hi, core = prompt // 4, (prompt // 2) % 2, prompt % 2
    z, x_lo = seq // 2, seq % 2
    parts = lax.axis_size("seq")
    width = queries.shape[2] // parts

    def to_heads(packed):
        heads = lax.all_to_all(packed, "seq", split_axis=0, concat_axis=0)
        return heads.reshape(-1, packed.shape[2])

    offsets, pieces = ring_z(context[0])
    both = jnp.concatenate([key_weight, value_weight], axis=1)
    packed = pack([queries[0], self_keys[0], self_values[0]], parts)
    chunk = gather_weights(both, packed[0], *pieces[-2:])
    qkv = to_heads(hold(packed, pieces[-3]))
    near, far = ring_y(chunk)
    text_rows = context.shape[1]
    mine, theirs = split_text(pieces, y, x_hi, core)
    other = lax.ppermute(theirs, "prompt", CORE_SWAP)
    other_parts = project(other, near, far)
    own_parts = lax.optimization_barrier(project(mine, near, far))
    own_columns, their_columns = [
        (own + lax.ppermute(part, "prompt", CORE_SWAP)).astype(jnp.bfloat16)
        for own, part in zip(own_parts, other_parts)
    ]
    swapped = lax.ppermute(their_columns, "seq", XL_SWAP)
    source_z = (z + jnp.array(offsets, jnp.int32)) % Z
    source_seq = jnp.stack([source_z * 2 + x_lo, source_z * 2 + 1 - x_lo]).reshape(-1, 1)
    slot = (source_seq * text_rows + jnp.arange(text_rows, dtype=jnp.int32)[None, :]).reshape(1, -1)
    bias = jnp.where(slot < lengths[0], 0.0, -jnp.inf).astype(jnp.float32)

    cq = to_heads(hold(pack([cross_queries[0]], parts), own_columns, their_columns))
    self_out = self_attend(qkv, width)
    text_kv = jnp.concatenate([own_columns, hold(swapped, self_out)], axis=0)
    attended = cross_attend(bias, cq, text_kv, self_out)
    back = lax.all_to_all(
        attended.reshape(parts, -1, width), "seq", split_axis=0, concat_axis=0
    )
    return unpack(back)[None]


def solution(mesh):
    in_specs = (
        P("prompt", "seq", None),
        P("prompt", "seq", None),
        P("prompt", "seq", None),
        P("prompt", "seq", None),
        P("prompt", "seq", None),
        P("prompt", "seq"),
        P("prompt", "seq"),
        P("prompt"),
    )
    out_specs = P("prompt", "seq", None)
    return jax.shard_map(body, mesh=mesh, in_specs=in_specs, out_specs=out_specs, check_vma=False)
```

```python
import functools
import math

import jax
import jax.numpy as jnp
from jax import lax
from jax.experimental import pallas as pl
from jax.experimental.pallas import tpu as pltpu
from jax.sharding import PartitionSpec as P

HD = 128
EXP2_SCALE = math.log2(math.e) / math.sqrt(HD)
Y, XH, CORE = 4, 2, 2
Z, XL = 8, 2


def y_shift(step):
    block = XH * CORE
    return [(p, (p + step * block) % (Y * block)) for p in range(Y * block)]


def z_shift(step):
    return [(s, (s + step * XL) % (Z * XL)) for s in range(Z * XL)]


SPLIT_FLOPS = 400_000_000_000
CORE_SWAP = [(p, p ^ 1) for p in range(Y * XH * CORE)]
XL_SWAP = [(s, s ^ 1) for s in range(Z * XL)]
XH_SWAP = [(p, p ^ 2) for p in range(Y * XH * CORE)]


def pack_kernel(width, parts, *refs):
    out_ref = refs[-1]
    for place, ref in enumerate(refs[:-1]):
        for part in range(parts):
            out_ref[part, :, place * width : (place + 1) * width] = ref[
                :, part * width : (part + 1) * width
            ]


def pack(arrays, parts):
    rows, columns = arrays[0].shape
    width = columns // parts
    block = math.gcd(rows, 64)
    return pl.pallas_call(
        functools.partial(pack_kernel, width, parts),
        grid=(rows // block,),
        in_specs=[pl.BlockSpec((block, columns), lambda i: (i, 0)) for _ in arrays],
        out_specs=pl.BlockSpec((parts, block, width * len(arrays)), lambda i: (0, i, 0)),
        out_shape=jax.ShapeDtypeStruct((parts, rows, width * len(arrays)), jnp.bfloat16),
        cost_estimate=pl.CostEstimate(
            flops=0, bytes_accessed=4 * rows * columns * len(arrays), transcendentals=0
        ),
        name="pack",
    )(*arrays)


def hold_kernel(*refs):
    del refs


def hold(array, *until):
    marks = [mark[:16, :HD] if mark.shape[0] > 16 else mark for mark in until]
    return pl.pallas_call(
        hold_kernel,
        in_specs=[pl.BlockSpec(memory_space=pl.ANY)] * (1 + len(marks)),
        out_specs=pl.BlockSpec(memory_space=pl.ANY),
        out_shape=jax.ShapeDtypeStruct(array.shape, array.dtype),
        input_output_aliases={0: 0},
        name="hold",
    )(array, *marks)


def unpack_kernel(in_ref, out_ref):
    parts, _, width = in_ref.shape
    for part in range(parts):
        out_ref[:, part * width : (part + 1) * width] = in_ref[part]


def unpack(blocks):
    parts, rows, width = blocks.shape
    block = math.gcd(rows, 64)
    return pl.pallas_call(
        unpack_kernel,
        grid=(rows // block,),
        in_specs=[pl.BlockSpec((parts, block, width), lambda i: (0, i, 0))],
        out_specs=pl.BlockSpec((block, parts * width), lambda i: (i, 0)),
        out_shape=jax.ShapeDtypeStruct((rows, parts * width), jnp.bfloat16),
        name="unpack",
    )(blocks)


def softmax_mix(query, keys, values, bias):
    scores = lax.dot_general(
        query, keys, (((1,), (1,)), ((), ())), preferred_element_type=jnp.float32
    )
    if bias is not None:
        scores = scores + bias
    row_max = jnp.max(scores, axis=1, keepdims=True)
    weights = jnp.exp2((scores - row_max) * EXP2_SCALE)
    totals = jnp.sum(weights, axis=1, keepdims=True)
    mixed = jnp.dot(weights.astype(jnp.bfloat16), values, preferred_element_type=jnp.float32)
    return mixed / totals


def self_kernel(q_ref, k_ref, v_ref, out_ref):
    rows = math.gcd(q_ref.shape[0], 256)
    for start in range(0, q_ref.shape[0], rows):
        for head in range(q_ref.shape[1] // HD):
            cols = slice(head * HD, (head + 1) * HD)
            out_ref[start : start + rows, cols] = softmax_mix(
                q_ref[start : start + rows, cols], k_ref[:, cols], v_ref[:, cols], None
            ).astype(jnp.bfloat16)


def cross_kernel(bias_ref, cq_ref, tk_ref, tv_ref, self_ref, out_ref):
    rows = math.gcd(cq_ref.shape[0], 512)
    for start in range(0, cq_ref.shape[0], rows):
        here = slice(start, start + rows)
        for head in range(cq_ref.shape[1] // HD):
            cols = slice(head * HD, (head + 1) * HD)
            cross_out = softmax_mix(
                cq_ref[here, cols], tk_ref[:, cols], tv_ref[:, cols], bias_ref[...]
            )
            out_ref[here, cols] = (
                self_ref[here, cols].astype(jnp.float32)
                + cross_out.astype(jnp.bfloat16).astype(jnp.float32)
            ).astype(jnp.bfloat16)


def self_attend(qkv, width):
    rows = qkv.shape[0]
    block = math.gcd(rows, 1024)
    pairs = rows * width * rows
    return pl.pallas_call(
        self_kernel,
        grid=(rows // block,),
        in_specs=[
            pl.BlockSpec((block, width), lambda i: (i, 0)),
            pl.BlockSpec((rows, width), lambda i: (0, 1)),
            pl.BlockSpec((rows, width), lambda i: (0, 2)),
        ],
        out_specs=pl.BlockSpec((block, width), lambda i: (i, 0)),
        out_shape=jax.ShapeDtypeStruct((rows, width), jnp.bfloat16),
        compiler_params=pltpu.CompilerParams(vmem_limit_bytes=40 << 20),
        cost_estimate=pl.CostEstimate(
            flops=4 * pairs, bytes_accessed=8 * rows * width, transcendentals=pairs // HD
        ),
        name="self_attend",
    )(qkv, qkv, qkv)


def cross_attend(bias, cq, text, self_out):
    rows, width = cq.shape
    slots = text.shape[0]
    block = math.gcd(rows, 1024)
    pairs = rows * width * slots
    row_spec = pl.BlockSpec((block, width), lambda i: (i, 0))
    return pl.pallas_call(
        cross_kernel,
        grid=(rows // block,),
        in_specs=[
            pl.BlockSpec((1, slots), lambda i: (0, 0)),
            row_spec,
            pl.BlockSpec((slots, width), lambda i: (0, 0)),
            pl.BlockSpec((slots, width), lambda i: (0, 1)),
            row_spec,
        ],
        out_specs=row_spec,
        out_shape=jax.ShapeDtypeStruct((rows, width), jnp.bfloat16),
        compiler_params=pltpu.CompilerParams(vmem_limit_bytes=32 << 20),
        cost_estimate=pl.CostEstimate(
            flops=4 * pairs, bytes_accessed=6 * rows * width, transcendentals=pairs // HD
        ),
        name="cross_attend",
    )(bias, cq, text, text, self_out)


def gather_weights(weights, early, *until):
    wide = jnp.concatenate([weights, lax.ppermute(weights, "seq", XL_SWAP)], axis=1)
    other = lax.ppermute(hold(wide, *early), "prompt", XH_SWAP)
    return jnp.concatenate([wide, hold(other, *until)], axis=0)


def ring_y(chunk):
    half = chunk.shape[1] // 2
    before = lax.ppermute(chunk, "prompt", y_shift(1))
    after = lax.ppermute(chunk, "prompt", y_shift(-1))
    far_left = lax.ppermute(before[:, :half], "prompt", y_shift(1))
    far_right = lax.ppermute(after[:, half:], "prompt", y_shift(-1))
    return (chunk, after, before), (far_left, far_right)


def project(text, near, far):
    deep, columns = near[0].shape
    chunks = [text[:, k * deep : (k + 1) * deep] for k in range(Y)]

    def dot(rows, weights):
        return jnp.dot(rows, weights, preferred_element_type=jnp.float32)

    sums = dot(chunks[0], near[0]) + dot(chunks[1], near[1]) + dot(chunks[3], near[2])
    sums = lax.optimization_barrier(sums)
    return [
        sums[:, : columns // 2] + dot(chunks[2], far[0]),
        sums[:, columns // 2 :] + dot(chunks[2], far[1]),
    ]


def ring_z(block):
    half = block.shape[0] // 2
    offsets, pieces = [0], [block]
    up = down = block
    for step in range(1, Z // 2):
        up = lax.ppermute(up, "seq", z_shift(1))
        down = lax.ppermute(down, "seq", z_shift(-1))
        offsets += [-step, step]
        pieces += [up, down]
    pieces.append(lax.ppermute(up[:half], "seq", z_shift(1)))
    pieces.append(lax.ppermute(down[half:], "seq", z_shift(-1)))
    return offsets + [Z // 2], pieces, down[half:]


def split_kernel(count, where_ref, *refs):
    outs = refs[count:]
    wide = refs[0].shape[1] // (XH * CORE)
    for x_hi in range(XH):
        for core in range(CORE):

            @pl.when((where_ref[1] == x_hi) & (where_ref[2] == core))
            def _():
                place = 0
                for ref in refs[:count]:
                    rows = slice(place, place + ref.shape[0])
                    for flip, out in enumerate(outs):
                        for k in range(XH):
                            chunk = (x_hi ^ k) * CORE + (core ^ flip)
                            out[rows, k * wide : (k + 1) * wide] = ref[
                                :, chunk * wide : (chunk + 1) * wide
                            ]
                    place += ref.shape[0]


def split_text(pieces, where):
    depth = pieces[0].shape[1]
    rows = sum(piece.shape[0] for piece in pieces)
    wide = depth // Y
    shape = jax.ShapeDtypeStruct((rows, depth // CORE), jnp.bfloat16)
    spec = pl.BlockSpec((rows, wide // CORE), lambda k, where: (0, k))
    return pl.pallas_call(
        functools.partial(split_kernel, len(pieces)),
        grid_spec=pltpu.PrefetchScalarGridSpec(
            num_scalar_prefetch=1,
            grid=(Y,),
            in_specs=[
                pl.BlockSpec((piece.shape[0], wide), lambda k, where: (0, (where[0] + k) % Y))
                for piece in pieces
            ],
            out_specs=[spec, spec],
        ),
        out_shape=[shape, shape],
        cost_estimate=pl.CostEstimate(
            flops=SPLIT_FLOPS, bytes_accessed=4 * rows * depth, transcendentals=0
        ),
        name="split_text",
    )(where, *pieces)


def body(
    queries, self_keys, self_values, cross_queries, context, key_weight, value_weight, lengths
):
    prompt, seq = lax.axis_index("prompt"), lax.axis_index("seq")
    y, x_hi, core = prompt // 4, (prompt // 2) % 2, prompt % 2
    z, x_lo = seq // 2, seq % 2
    parts = lax.axis_size("seq")
    width = queries.shape[2] // parts

    def to_heads(packed):
        heads = lax.all_to_all(packed, "seq", split_axis=0, concat_axis=0)
        return heads.reshape(-1, packed.shape[2])

    offsets, pieces, sent = ring_z(context[0])
    both = jnp.concatenate([key_weight, value_weight], axis=1)
    packed = pack([queries[0], self_keys[0], self_values[0]], parts)
    where = jnp.stack([y, x_hi, core])
    chunk = gather_weights(both, (packed[0], where), *pieces[-2:])
    qkv = to_heads(hold(packed, sent))
    near, far = ring_y(chunk)
    text_rows = context.shape[1]
    mine, theirs = split_text(pieces, where)
    other = lax.ppermute(theirs, "prompt", CORE_SWAP)
    other_parts = project(other, near, far)
    own_parts = lax.optimization_barrier(project(mine, near, far))
    own_columns, their_columns = [
        (own + lax.ppermute(part, "prompt", CORE_SWAP)).astype(jnp.bfloat16)
        for own, part in zip(own_parts, other_parts)
    ]
    swapped = lax.ppermute(their_columns, "seq", XL_SWAP)
    source_z = (z + jnp.array(offsets, jnp.int32)) % Z
    source_seq = jnp.stack([source_z * 2 + x_lo, source_z * 2 + 1 - x_lo]).reshape(-1, 1)
    slot = (source_seq * text_rows + jnp.arange(text_rows, dtype=jnp.int32)[None, :]).reshape(1, -1)
    bias = jnp.where(slot < lengths[0], 0.0, -jnp.inf).astype(jnp.float32)

    cq = to_heads(hold(pack([cross_queries[0]], parts), own_columns, their_columns))
    self_out = self_attend(qkv, width)
    text_kv = jnp.concatenate([own_columns, hold(swapped, self_out)], axis=0)
    attended = cross_attend(bias, cq, text_kv, self_out)
    back = lax.all_to_all(
        attended.reshape(parts, -1, width), "seq", split_axis=0, concat_axis=0
    )
    return unpack(back)[None]


def solution(mesh):
    in_specs = (
        P("prompt", "seq", None),
        P("prompt", "seq", None),
        P("prompt", "seq", None),
        P("prompt", "seq", None),
        P("prompt", "seq", None),
        P("prompt", "seq"),
        P("prompt", "seq"),
        P("prompt"),
    )
    out_specs = P("prompt", "seq", None)
    return jax.shard_map(body, mesh=mesh, in_specs=in_specs, out_specs=out_specs, check_vma=False)
```

```python
import functools
import math

import jax
import jax.numpy as jnp
from jax import lax
from jax.experimental import pallas as pl
from jax.experimental.pallas import tpu as pltpu
from jax.sharding import PartitionSpec as P

HD = 128
EXP2_SCALE = math.log2(math.e) / math.sqrt(HD)
Y, XH, CORE = 4, 2, 2
Z, XL = 8, 2


def y_shift(step):
    block = XH * CORE
    return [(p, (p + step * block) % (Y * block)) for p in range(Y * block)]


def z_shift(step):
    return [(s, (s + step * XL) % (Z * XL)) for s in range(Z * XL)]


SPLIT_FLOPS = 400_000_000_000
CORE_SWAP = [(p, p ^ 1) for p in range(Y * XH * CORE)]
XL_SWAP = [(s, s ^ 1) for s in range(Z * XL)]
XH_SWAP = [(p, p ^ 2) for p in range(Y * XH * CORE)]


def pack_kernel(width, parts, *refs):
    out_ref = refs[-1]
    for place, ref in enumerate(refs[:-1]):
        for part in range(parts):
            out_ref[part, :, place * width : (place + 1) * width] = ref[
                :, part * width : (part + 1) * width
            ]


def pack(arrays, parts):
    rows, columns = arrays[0].shape
    width = columns // parts
    block = math.gcd(rows, 64)
    return pl.pallas_call(
        functools.partial(pack_kernel, width, parts),
        grid=(rows // block,),
        in_specs=[pl.BlockSpec((block, columns), lambda i: (i, 0)) for _ in arrays],
        out_specs=pl.BlockSpec((parts, block, width * len(arrays)), lambda i: (0, i, 0)),
        out_shape=jax.ShapeDtypeStruct((parts, rows, width * len(arrays)), jnp.bfloat16),
        cost_estimate=pl.CostEstimate(
            flops=0, bytes_accessed=4 * rows * columns * len(arrays), transcendentals=0
        ),
        name="pack",
    )(*arrays)


def hold_kernel(*refs):
    del refs


def hold(array, *until):
    marks = [mark[:16, :HD] if mark.shape[0] > 16 else mark for mark in until]
    return pl.pallas_call(
        hold_kernel,
        in_specs=[pl.BlockSpec(memory_space=pl.ANY)] * (1 + len(marks)),
        out_specs=pl.BlockSpec(memory_space=pl.ANY),
        out_shape=jax.ShapeDtypeStruct(array.shape, array.dtype),
        input_output_aliases={0: 0},
        name="hold",
    )(array, *marks)


def unpack_kernel(in_ref, out_ref):
    parts, _, width = in_ref.shape
    for part in range(parts):
        out_ref[:, part * width : (part + 1) * width] = in_ref[part]


def unpack(blocks):
    parts, rows, width = blocks.shape
    block = math.gcd(rows, 64)
    return pl.pallas_call(
        unpack_kernel,
        grid=(rows // block,),
        in_specs=[pl.BlockSpec((parts, block, width), lambda i: (0, i, 0))],
        out_specs=pl.BlockSpec((block, parts * width), lambda i: (i, 0)),
        out_shape=jax.ShapeDtypeStruct((rows, parts * width), jnp.bfloat16),
        name="unpack",
    )(blocks)


def softmax_mix(query, keys, values, bias):
    scores = lax.dot_general(
        query, keys, (((1,), (1,)), ((), ())), preferred_element_type=jnp.float32
    )
    if bias is not None:
        scores = scores + bias
    row_max = jnp.max(scores, axis=1, keepdims=True)
    weights = jnp.exp2((scores - row_max) * EXP2_SCALE)
    totals = jnp.sum(weights, axis=1, keepdims=True)
    mixed = jnp.dot(weights.astype(jnp.bfloat16), values, preferred_element_type=jnp.float32)
    return mixed / totals


def self_kernel(q_ref, k_ref, v_ref, out_ref):
    rows = math.gcd(q_ref.shape[0], 256)
    for start in range(0, q_ref.shape[0], rows):
        for head in range(q_ref.shape[1] // HD):
            cols = slice(head * HD, (head + 1) * HD)
            out_ref[start : start + rows, cols] = softmax_mix(
                q_ref[start : start + rows, cols], k_ref[:, cols], v_ref[:, cols], None
            ).astype(jnp.bfloat16)


def cross_kernel(bias_ref, cq_ref, tk_ref, tv_ref, self_ref, out_ref):
    rows = math.gcd(cq_ref.shape[0], 512)
    for start in range(0, cq_ref.shape[0], rows):
        here = slice(start, start + rows)
        for head in range(cq_ref.shape[1] // HD):
            cols = slice(head * HD, (head + 1) * HD)
            cross_out = softmax_mix(
                cq_ref[here, cols], tk_ref[:, cols], tv_ref[:, cols], bias_ref[...]
            )
            out_ref[here, cols] = (
                self_ref[here, cols].astype(jnp.float32)
                + cross_out.astype(jnp.bfloat16).astype(jnp.float32)
            ).astype(jnp.bfloat16)


def self_attend(qkv, width):
    rows = qkv.shape[0]
    block = math.gcd(rows, 1024)
    pairs = rows * width * rows
    return pl.pallas_call(
        self_kernel,
        grid=(rows // block,),
        in_specs=[
            pl.BlockSpec((block, width), lambda i: (i, 0)),
            pl.BlockSpec((rows, width), lambda i: (0, 1)),
            pl.BlockSpec((rows, width), lambda i: (0, 2)),
        ],
        out_specs=pl.BlockSpec((block, width), lambda i: (i, 0)),
        out_shape=jax.ShapeDtypeStruct((rows, width), jnp.bfloat16),
        compiler_params=pltpu.CompilerParams(vmem_limit_bytes=40 << 20),
        cost_estimate=pl.CostEstimate(
            flops=4 * pairs, bytes_accessed=8 * rows * width, transcendentals=pairs // HD
        ),
        name="self_attend",
    )(qkv, qkv, qkv)


def cross_attend(bias, cq, text, self_out):
    rows, width = cq.shape
    slots = text.shape[0]
    block = math.gcd(rows, 2048)
    pairs = rows * width * slots
    row_spec = pl.BlockSpec((block, width), lambda i: (i, 0))
    return pl.pallas_call(
        cross_kernel,
        grid=(rows // block,),
        in_specs=[
            pl.BlockSpec((1, slots), lambda i: (0, 0)),
            row_spec,
            pl.BlockSpec((slots, width), lambda i: (0, 0)),
            pl.BlockSpec((slots, width), lambda i: (0, 1)),
            row_spec,
        ],
        out_specs=row_spec,
        out_shape=jax.ShapeDtypeStruct((rows, width), jnp.bfloat16),
        compiler_params=pltpu.CompilerParams(vmem_limit_bytes=32 << 20),
        cost_estimate=pl.CostEstimate(
            flops=4 * pairs, bytes_accessed=6 * rows * width, transcendentals=pairs // HD
        ),
        name="cross_attend",
    )(bias, cq, text, text, self_out)


def gather_weights(weights, early, *until):
    wide = jnp.concatenate([weights, lax.ppermute(weights, "seq", XL_SWAP)], axis=1)
    other = lax.ppermute(hold(wide, *early), "prompt", XH_SWAP)
    return jnp.concatenate([wide, hold(other, *until)], axis=0)


def ring_y(chunk):
    half = chunk.shape[1] // 2
    before = lax.ppermute(chunk, "prompt", y_shift(1))
    after = lax.ppermute(chunk, "prompt", y_shift(-1))
    far_left = lax.ppermute(before[:, :half], "prompt", y_shift(1))
    far_right = lax.ppermute(after[:, half:], "prompt", y_shift(-1))
    return (chunk, after, before), (far_left, far_right)


def project(text, near, far):
    deep, columns = near[0].shape
    chunks = [text[:, k * deep : (k + 1) * deep] for k in range(Y)]

    def dot(rows, weights):
        return jnp.dot(rows, weights, preferred_element_type=jnp.float32)

    sums = dot(chunks[0], near[0]) + dot(chunks[1], near[1]) + dot(chunks[3], near[2])
    sums = lax.optimization_barrier(sums)
    return [
        sums[:, : columns // 2] + dot(chunks[2], far[0]),
        sums[:, columns // 2 :] + dot(chunks[2], far[1]),
    ]


def ring_z(block):
    half = block.shape[0] // 2
    offsets, pieces = [0], [block]
    up = down = block
    for step in range(1, Z // 2):
        up = lax.ppermute(up, "seq", z_shift(1))
        down = lax.ppermute(down, "seq", z_shift(-1))
        offsets += [-step, step]
        pieces += [up, down]
    pieces.append(lax.ppermute(up[:half], "seq", z_shift(1)))
    pieces.append(lax.ppermute(down[half:], "seq", z_shift(-1)))
    return offsets + [Z // 2], pieces, down[half:]


def split_kernel(count, where_ref, *refs):
    outs = refs[count:]
    wide = refs[0].shape[1] // (XH * CORE)
    for x_hi in range(XH):
        for core in range(CORE):

            @pl.when((where_ref[1] == x_hi) & (where_ref[2] == core))
            def _():
                place = 0
                for ref in refs[:count]:
                    rows = slice(place, place + ref.shape[0])
                    for flip, out in enumerate(outs):
                        for k in range(XH):
                            chunk = (x_hi ^ k) * CORE + (core ^ flip)
                            out[rows, k * wide : (k + 1) * wide] = ref[
                                :, chunk * wide : (chunk + 1) * wide
                            ]
                    place += ref.shape[0]


def split_text(pieces, where):
    depth = pieces[0].shape[1]
    rows = sum(piece.shape[0] for piece in pieces)
    wide = depth // Y
    shape = jax.ShapeDtypeStruct((rows, depth // CORE), jnp.bfloat16)
    spec = pl.BlockSpec((rows, wide // CORE), lambda k, where: (0, k))
    return pl.pallas_call(
        functools.partial(split_kernel, len(pieces)),
        grid_spec=pltpu.PrefetchScalarGridSpec(
            num_scalar_prefetch=1,
            grid=(Y,),
            in_specs=[
                pl.BlockSpec((piece.shape[0], wide), lambda k, where: (0, (where[0] + k) % Y))
                for piece in pieces
            ],
            out_specs=[spec, spec],
        ),
        out_shape=[shape, shape],
        cost_estimate=pl.CostEstimate(
            flops=SPLIT_FLOPS, bytes_accessed=4 * rows * depth, transcendentals=0
        ),
        name="split_text",
    )(where, *pieces)


def body(
    queries, self_keys, self_values, cross_queries, context, key_weight, value_weight, lengths
):
    prompt, seq = lax.axis_index("prompt"), lax.axis_index("seq")
    y, x_hi, core = prompt // 4, (prompt // 2) % 2, prompt % 2
    z, x_lo = seq // 2, seq % 2
    parts = lax.axis_size("seq")
    width = queries.shape[2] // parts

    def to_heads(packed):
        heads = lax.all_to_all(packed, "seq", split_axis=0, concat_axis=0)
        return heads.reshape(-1, packed.shape[2])

    offsets, pieces, sent = ring_z(context[0])
    both = jnp.concatenate([key_weight, value_weight], axis=1)
    packed = pack([queries[0], self_keys[0], self_values[0]], parts)
    where = jnp.stack([y, x_hi, core])
    chunk = gather_weights(both, (packed[0], where), *pieces[-2:])
    qkv = to_heads(hold(packed, sent))
    near, far = ring_y(chunk)
    text_rows = context.shape[1]
    mine, theirs = split_text(pieces, where)
    other = lax.ppermute(theirs, "prompt", CORE_SWAP)
    other_parts = project(other, near, far)
    own_parts = lax.optimization_barrier(project(mine, near, far))
    own_columns, their_columns = [
        (own + lax.ppermute(part, "prompt", CORE_SWAP)).astype(jnp.bfloat16)
        for own, part in zip(own_parts, other_parts)
    ]
    swapped = lax.ppermute(their_columns, "seq", XL_SWAP)
    source_z = (z + jnp.array(offsets, jnp.int32)) % Z
    source_seq = jnp.stack([source_z * 2 + x_lo, source_z * 2 + 1 - x_lo]).reshape(-1, 1)
    slot = (source_seq * text_rows + jnp.arange(text_rows, dtype=jnp.int32)[None, :]).reshape(1, -1)
    bias = jnp.where(slot < lengths[0], 0.0, -jnp.inf).astype(jnp.float32)

    cq = to_heads(hold(pack([cross_queries[0]], parts), own_columns, their_columns))
    self_out = self_attend(qkv, width)
    text_kv = jnp.concatenate([own_columns, hold(swapped, self_out)], axis=0)
    attended = cross_attend(bias, cq, text_kv, self_out)
    back = lax.all_to_all(
        attended.reshape(parts, -1, width), "seq", split_axis=0, concat_axis=0
    )
    return unpack(back)[None]


def solution(mesh):
    in_specs = (
        P("prompt", "seq", None),
        P("prompt", "seq", None),
        P("prompt", "seq", None),
        P("prompt", "seq", None),
        P("prompt", "seq", None),
        P("prompt", "seq"),
        P("prompt", "seq"),
        P("prompt"),
    )
    out_specs = P("prompt", "seq", None)
    return jax.shard_map(body, mesh=mesh, in_specs=in_specs, out_specs=out_specs, check_vma=False)
```
